32 devices in a mesh: seq: 4 (over y, x), dp: 8 (over z, core).
Axes of the slice: x: 2, y: 2, z: 4, core: 2. Of those that a mesh axis runs over, the one named last changes fastest.
Arguments:
- query_rows: bfloat16 [8, 1024, 2048], P('dp', 'seq'), may hold values from -22 to 22
- key_rows: bfloat16 [8, 1024, 2048], P('dp', 'seq'), may hold values from -7 to 7
- value_rows: bfloat16 [8, 1024, 2048], P('dp', 'seq'), may hold values from -6 to 6
- sink_logit: float32 [16], replicated, may hold values from 6 to 11
- grad_out: bfloat16 [8, 1024, 2048], P('dp', 'seq'), may hold values from -1.6 to 1.6
- pattern: int32 [16, 8, 8], replicated, may hold values from 0 to 7, as said below
Outputs:
- attended: bfloat16 [8, 1024, 2048], P('dp', 'seq')
- grad_query: bfloat16 [8, 1024, 2048], P('dp', 'seq')
- grad_key: bfloat16 [8, 1024, 2048], P('dp', 'seq')
- grad_value: bfloat16 [8, 1024, 2048], P('dp', 'seq')
- grad_sink: float32 [16], replicated
The draws below stay inside these ranges and needn't reach their ends.
Inputs may be any that keep to these rules, and one draw needn't show every extreme that they name: For each head h and query block b, pattern[h, b] lists 8 distinct key blocks: the three neighbouring blocks b - 1, b, b + 1 (moved inward at the ends of the document), the first and the last block, and blocks drawn at random to fill the row.
All inputs are finite; a program needn't handle non-finite values.
Results may differ from the reference program's by a relative error of at most 0.012.
The reference program's roundings to bfloat16 on the way count: a program that leaves them out, or rounds other values in their place, can miss the bound.
Values may be sent and summed in bfloat16 or wider, within the bound.
A program may use at most 64 MiB of HBM per device.

```python
import jax
import jax.numpy as jnp
from jax import lax

H = 16
HEAD = 128
BLOCK = 128
KB = 8
DOCS = 8
SEQLEN = 1024
NB = 8


def base_keys(key):
    shape = (DOCS, SEQLEN, H * HEAD)
    return jnp.clip(jax.random.normal(jax.random.fold_in(key, 7), shape, jnp.float32), -4.0, 4.0)


def draw_key_rows(key, part):
    return base_keys(key).astype(jnp.bfloat16)


def draw_query_rows(key, part):
    shape = (DOCS, SEQLEN, H * HEAD)
    raw = jnp.clip(jax.random.normal(jax.random.fold_in(key, 21), shape, jnp.float32), -4.0, 4.0)
    return (2.5 * raw).astype(jnp.bfloat16)


def draw_grad_out(key, part):
    shape = (DOCS, SEQLEN, H * HEAD)
    rising = jnp.arange(DOCS, dtype=jnp.float32)[:, None, None] / max(DOCS - 1, 1)
    raw = jnp.clip(jax.random.normal(jax.random.fold_in(key, 31), shape, jnp.float32), -4.0, 4.0)
    return (0.1 * (1.0 + 2.0 * rising) * raw).astype(jnp.bfloat16)


def draw_pattern(key, part):
    blocks = jnp.arange(NB)
    start = jnp.clip(blocks - 1, 0, NB - 3)
    window = (blocks[None, :] >= start[:, None]) & (blocks[None, :] < start[:, None] + 3)
    globe = (blocks == 0) | (blocks == NB - 1)
    special = (window | globe[None, :]).astype(jnp.int32)
    subkeys = jax.random.split(jax.random.fold_in(key, 41), H * NB)
    orders = jax.vmap(lambda single: jax.random.permutation(single, NB))(subkeys).reshape(H, NB, NB)
    ranking = special[None, :, :] * (2 * NB) + orders.astype(jnp.int32)
    _, chosen = lax.top_k(ranking, KB)
    return chosen.astype(jnp.int32)


def levels(rng, dims, shards, least, largest):
    factor_of = 1.0
    for position, shards_of in shards:
        heights = jax.random.uniform(jax.random.fold_in(jax.random.fold_in(rng, 6), position), (shards_of,), jnp.float32, least / len(shards), largest / len(shards))
        factor_of = factor_of * jnp.repeat(jnp.exp(heights), dims[position] // shards_of).reshape((-1,) + (1,) * (len(dims) - 1 - position))
    return factor_of


def centred(key, shape, spread, reach, shards=(), kind=jnp.bfloat16):
    array = spread * jax.random.normal(key, shape, jnp.float32)
    if shards:
        array = array * levels(key, shape, shards, -0.22, 0.18)
    return jnp.clip(array, -reach, reach).astype(kind)


def setup_inputs(seed: int = 0) -> dict:
    key_of = jax.random.split(jax.random.key(seed), 7)
    query_rows = draw_query_rows(jax.random.fold_in(key_of[6], 71), 0)
    key_rows = draw_key_rows(jax.random.fold_in(key_of[6], 71), 0)
    value_rows = centred(key_of[2], (DOCS, SEQLEN, H * HEAD), 1.0, 6.0, ((0, 8), (1, 4)))
    sink_logit = jnp.clip(jax.random.uniform(key_of[3], (H,), jnp.float32, 6.0, 11.0), 6.0, 11.0)
    grad_out = draw_grad_out(jax.random.fold_in(key_of[6], 71), 0)
    pattern = draw_pattern(jax.random.fold_in(key_of[6], 71), 0)
    return dict(query_rows=query_rows, key_rows=key_rows, value_rows=value_rows, sink_logit=sink_logit, grad_out=grad_out, pattern=pattern)


def head_pass(query_head, key_head, value_head, grad_head, link_rows, sink_value):
    block_count = query_head.shape[0] // BLOCK
    scaling = HEAD ** -0.5
    queries = query_head.reshape(block_count, BLOCK, HEAD).astype(jnp.float32)
    key_tiles = key_head.reshape(block_count, BLOCK, HEAD)[link_rows].astype(jnp.float32)
    value_tiles = value_head.reshape(block_count, BLOCK, HEAD)[link_rows].astype(jnp.float32)
    grads = grad_head.reshape(block_count, BLOCK, HEAD).astype(jnp.float32)
    scores = jnp.einsum("nqe,nkbe->nqkb", queries, key_tiles) * scaling
    row_top = jnp.maximum(jnp.max(scores, axis=(2, 3)), sink_value)
    summed = jnp.sum(jnp.exp(scores - row_top[:, :, None, None]), axis=(2, 3)) + jnp.exp(sink_value - row_top)
    log_total = row_top + jnp.log(summed)
    weights = jnp.exp(scores - log_total[:, :, None, None])
    rounded = lax.optimization_barrier(weights.astype(jnp.bfloat16)).astype(jnp.float32)
    attended = jnp.einsum("nqkb,nkbe->nqe", rounded, value_tiles).astype(jnp.bfloat16)
    attended_wide = lax.optimization_barrier(attended).astype(jnp.float32)
    row_dot = jnp.sum(grads * attended_wide, axis=-1)
    grad_weights = jnp.einsum("nqe,nkbe->nqkb", grads, value_tiles)
    grad_scores = (weights * (grad_weights - row_dot[:, :, None, None])).astype(jnp.bfloat16)
    grad_scores = lax.optimization_barrier(grad_scores).astype(jnp.float32)
    grad_query = (jnp.einsum("nqkb,nkbe->nqe", grad_scores, key_tiles) * scaling).astype(jnp.bfloat16)
    key_part = jnp.einsum("nqkb,nqe->nkbe", grad_scores, queries) * scaling
    value_part = jnp.einsum("nqkb,nqe->nkbe", rounded, grads)
    flat_links = link_rows.reshape(-1).astype(jnp.int32)
    grad_key = jnp.zeros((block_count, BLOCK, HEAD), jnp.float32).at[flat_links].add(key_part.reshape(-1, BLOCK, HEAD))
    grad_value = jnp.zeros((block_count, BLOCK, HEAD), jnp.float32).at[flat_links].add(value_part.reshape(-1, BLOCK, HEAD))
    sink_term = -jnp.sum(jnp.exp(sink_value - log_total) * row_dot)
    return (attended.reshape(-1, HEAD), grad_query.reshape(-1, HEAD),
            grad_key.astype(jnp.bfloat16).reshape(-1, HEAD), grad_value.astype(jnp.bfloat16).reshape(-1, HEAD), sink_term)


def by_head(array_in):
    return jnp.transpose(array_in.reshape(SEQLEN, H, HEAD), (1, 0, 2))


def by_token(array_in):
    return jnp.transpose(array_in, (1, 0, 2)).reshape(SEQLEN, H * HEAD)


def reference(query_rows, key_rows, value_rows, sink_logit, grad_out, pattern):
    def per_document(inputs):
        query_doc, key_doc, value_doc, grad_doc = inputs
        results = lax.map(lambda packed: head_pass(*packed),
                          (by_head(query_doc), by_head(key_doc), by_head(value_doc), by_head(grad_doc), pattern, sink_logit))
        return by_token(results[0]), by_token(results[1]), by_token(results[2]), by_token(results[3]), results[4]

    outputs = lax.map(per_document, (query_rows, key_rows, value_rows, grad_out))
    grad_sink = jnp.sum(outputs[4], axis=0) / DOCS
    return outputs[0], outputs[1], outputs[2], outputs[3], grad_sink
```

```python
import functools

import jax
import jax.numpy as jnp
from jax import lax
from jax.experimental import pallas as pl
from jax.experimental.pallas import tpu as pltpu
from jax.sharding import PartitionSpec as P

MESH = pl.DeviceIdType.MESH

HEAD = 128
BLOCK = 128
CHUNK = 256


tile_group = 4


def tile_scores(queries, key_tiles, scaling):
    return (
        jnp.einsum("gqe,gkbe->gqkb", queries, key_tiles, preferred_element_type=jnp.float32)
        * scaling
    )


def log_totals(scores, sink_value):
    row_top = jnp.maximum(jnp.max(scores, axis=(2, 3)), sink_value)
    summed = jnp.sum(jnp.exp(scores - row_top[:, :, None, None]), axis=(2, 3)) + jnp.exp(
        sink_value - row_top
    )
    return row_top + jnp.log(summed)


def softmax_weights(scores, log_total):
    weights = jnp.exp(scores - log_total[:, :, None, None])
    return (weights, weights.astype(jnp.bfloat16))


def attend(rounded, value_tiles):
    return jnp.einsum(
        "gqkb,gkbe->gqe", rounded, value_tiles, preferred_element_type=jnp.float32
    ).astype(jnp.bfloat16)


def gradients(
    weights,
    rounded,
    attended,
    queries,
    key_tiles,
    value_tiles,
    grad_tile,
    log_total,
    sink_value,
    scaling,
):
    row_dot = jnp.sum(grad_tile.astype(jnp.float32) * attended.astype(jnp.float32), axis=-1)
    grad_weights = jnp.einsum(
        "gqe,gkbe->gqkb", grad_tile, value_tiles, preferred_element_type=jnp.float32
    )
    grad_scores = (weights * (grad_weights - row_dot[:, :, None, None])).astype(jnp.bfloat16)
    grad_query = (
        jnp.einsum("gqkb,gkbe->gqe", grad_scores, key_tiles, preferred_element_type=jnp.float32)
        * scaling
    ).astype(jnp.bfloat16)
    key_part = (
        jnp.einsum("gqkb,gqe->gkbe", grad_scores, queries, preferred_element_type=jnp.float32)
        * scaling
    )
    value_part = jnp.einsum(
        "gqkb,gqe->gkbe", rounded, grad_tile, preferred_element_type=jnp.float32
    )
    sink_part = -jnp.sum(jnp.exp(sink_value - log_total) * row_dot)
    return (grad_query, key_part, value_part, sink_part)


def head_tiles(array_in, head_index):
    row_count = array_in.shape[0]
    picked = lax.dynamic_index_in_dim(array_in, head_index, 1, keepdims=False)
    return picked.reshape(row_count // BLOCK, BLOCK, HEAD)


def put_head(buffer, tiles, head_index):
    return lax.dynamic_update_slice_in_dim(buffer, tiles.reshape(-1, 1, HEAD), head_index, 1)


def group_rows(tiles, group_index):
    return lax.dynamic_slice_in_dim(tiles, group_index * tile_group, tile_group, 0)


def put_group(buffer, tiles, group_index):
    return lax.dynamic_update_slice_in_dim(buffer, tiles, group_index * tile_group, 0)


def put_scalar(buffer, value_in, head_index):
    return lax.dynamic_update_slice_in_dim(buffer, value_in[None], head_index, 0)


def forward_pass(query_heads, key_heads, value_heads, head_links, head_sinks, scaling):
    row_count, local_heads, _ = query_heads.shape
    block_count = row_count // BLOCK

    def forward_one_head(head_index, head_state):
        attended, log_total = head_state
        query_tiles = head_tiles(query_heads, head_index)
        key_all = head_tiles(key_heads, head_index)
        value_all = head_tiles(value_heads, head_index)
        link_rows = lax.dynamic_index_in_dim(head_links, head_index, 0, keepdims=False)
        sink_value = lax.dynamic_index_in_dim(head_sinks, head_index, 0, keepdims=False)

        def forward_one_group(group_index, inner_state):
            out_tiles, total_tiles = inner_state
            chosen = group_rows(link_rows, group_index)
            scores = tile_scores(group_rows(query_tiles, group_index), key_all[chosen], scaling)
            group_total = log_totals(scores, sink_value)
            _, rounded = softmax_weights(scores, group_total)
            result = attend(rounded, value_all[chosen])
            return (
                put_group(out_tiles, result, group_index),
                put_group(total_tiles, group_total, group_index),
            )

        initial = (
            jnp.zeros((block_count, BLOCK, HEAD), jnp.bfloat16),
            jnp.zeros((block_count, BLOCK), jnp.float32),
        )
        out_tiles, total_tiles = lax.fori_loop(
            0, block_count // tile_group, forward_one_group, initial
        )
        return (
            put_head(attended, out_tiles, head_index),
            lax.dynamic_update_slice_in_dim(log_total, total_tiles[None], head_index, 0),
        )

    initial = (
        jnp.zeros((row_count, local_heads, HEAD), jnp.bfloat16),
        jnp.zeros((local_heads, block_count, BLOCK), jnp.float32),
    )
    return lax.fori_loop(0, local_heads, forward_one_head, initial)


def backward_pass(
    query_heads,
    key_heads,
    value_heads,
    grad_heads,
    attended,
    log_total,
    head_links,
    head_sinks,
    scaling,
):
    row_count, local_heads, _ = query_heads.shape
    block_count = row_count // BLOCK

    def backward_one_head(head_index, head_state):
        query_grads, key_grads, value_grads, sink_terms = head_state
        query_tiles = head_tiles(query_heads, head_index)
        key_all = head_tiles(key_heads, head_index)
        value_all = head_tiles(value_heads, head_index)
        grad_tiles = head_tiles(grad_heads, head_index)
        out_tiles = head_tiles(attended, head_index)
        head_total = lax.dynamic_index_in_dim(log_total, head_index, 0, keepdims=False)
        link_rows = lax.dynamic_index_in_dim(head_links, head_index, 0, keepdims=False)
        sink_value = lax.dynamic_index_in_dim(head_sinks, head_index, 0, keepdims=False)

        def backward_one_group(group_index, inner_state):
            query_part_all, key_acc, value_acc, sink_acc = inner_state
            chosen = group_rows(link_rows, group_index)
            queries = group_rows(query_tiles, group_index)
            key_tiles = key_all[chosen]
            value_tiles = value_all[chosen]
            group_total = group_rows(head_total, group_index)
            scores = tile_scores(queries, key_tiles, scaling)
            weights, rounded = softmax_weights(scores, group_total)
            grad_query, key_part, value_part, sink_part = gradients(
                weights,
                rounded,
                group_rows(out_tiles, group_index),
                queries,
                key_tiles,
                value_tiles,
                group_rows(grad_tiles, group_index),
                group_total,
                sink_value,
                scaling,
            )
            flat_links = chosen.reshape(-1)
            key_acc = key_acc.at[flat_links].add(key_part.reshape(-1, BLOCK, HEAD))
            value_acc = value_acc.at[flat_links].add(value_part.reshape(-1, BLOCK, HEAD))
            return (
                put_group(query_part_all, grad_query, group_index),
                key_acc,
                value_acc,
                sink_acc + sink_part,
            )

        initial = (
            jnp.zeros((block_count, BLOCK, HEAD), jnp.bfloat16),
            jnp.zeros((block_count, BLOCK, HEAD), jnp.float32),
            jnp.zeros((block_count, BLOCK, HEAD), jnp.float32),
            jnp.zeros((), jnp.float32),
        )
        query_part_all, key_acc, value_acc, sink_acc = lax.fori_loop(
            0, block_count // tile_group, backward_one_group, initial
        )
        return (
            put_head(query_grads, query_part_all, head_index),
            put_head(key_grads, key_acc.astype(jnp.bfloat16), head_index),
            put_head(value_grads, value_acc.astype(jnp.bfloat16), head_index),
            put_scalar(sink_terms, sink_acc, head_index),
        )

    blank = jnp.zeros((row_count, local_heads, HEAD), jnp.bfloat16)
    initial = (blank, blank, blank, jnp.zeros((local_heads,), jnp.float32))
    return lax.fori_loop(0, local_heads, backward_one_head, initial)


def exchange_kernel(
    n,
    local_heads,
    scaling,
    query_ref,
    key_ref,
    value_ref,
    grad_ref,
    sink_ref,
    attended_ref,
    query_grad_ref,
    key_grad_ref,
    value_grad_ref,
    sink_out_ref,
    held,
    made,
    key_acc,
    value_acc,
    own_in,
    own_out,
    in_send,
    in_recv,
    out_send,
    out_recv,
):
    me = lax.axis_index("seq")
    rows = query_ref.shape[0]
    total_rows = held.shape[2]
    given = (query_ref, key_ref, value_ref, grad_ref)
    wanted = (attended_ref, query_grad_ref, key_grad_ref, value_grad_ref)

    def partner(step):
        return lax.rem(me + step, n)

    def columns(device, head):
        return pl.ds(pl.multiple_of((device * local_heads + head) * HEAD, HEAD), HEAD)

    def row_range(device):
        return pl.ds(pl.multiple_of(device * rows, rows), rows)

    def copies_in(head):
        own, remote = [], []
        for which, source in enumerate(given):
            own.append(
                pltpu.make_async_copy(
                    source.at[:, columns(me, head)],
                    held.at[which, head, row_range(me)],
                    own_in.at[head, which],
                )
            )
            for step in range(1, n):
                to = partner(step)
                remote.append(
                    pltpu.make_async_remote_copy(
                        src_ref=source.at[:, columns(to, head)],
                        dst_ref=held.at[which, head, row_range(me)],
                        send_sem=in_send.at[head, which, step - 1],
                        recv_sem=in_recv.at[head, which, step - 1],
                        device_id={"seq": to},
                        device_id_type=MESH,
                    )
                )
        return own, remote

    def copies_out(head):
        own, remote = [], []
        for which, target in enumerate(wanted):
            own.append(
                pltpu.make_async_copy(
                    made.at[which, head, row_range(me)],
                    target.at[:, columns(me, head)],
                    own_out.at[head, which],
                )
            )
            for step in range(1, n):
                to = partner(step)
                remote.append(
                    pltpu.make_async_remote_copy(
                        src_ref=made.at[which, head, row_range(to)],
                        dst_ref=target.at[:, columns(me, head)],
                        send_sem=out_send.at[head, which, step - 1],
                        recv_sem=out_recv.at[head, which, step - 1],
                        device_id={"seq": to},
                        device_id_type=MESH,
                    )
                )
        return own, remote

    def start_all(copies):
        own, remote = copies
        for copy in remote + own:
            copy.start()

    barrier = pltpu.get_barrier_semaphore()
    for step in range(1, n):
        pl.semaphore_signal(
            barrier, inc=1, device_id={"seq": partner(step)}, device_id_type=MESH
        )
    pl.semaphore_wait(barrier, n - 1)

    start_all(copies_in(0))
    if local_heads > 1:
        start_all(copies_in(1))
    sink_out_ref[...] = jnp.zeros_like(sink_out_ref)
    lanes = lax.broadcasted_iota(jnp.int32, sink_out_ref.shape, 1)

    def one_head(head, carry):
        own, remote = copies_in(head)
        for copy in own:
            copy.wait()
        for copy in remote:
            copy.wait_recv()

        @pl.when(head + 2 < local_heads)
        def _():
            start_all(copies_in(head + 2))

        sink_value = sink_ref[me * local_heads + head]
        key_acc[...] = jnp.zeros_like(key_acc)
        value_acc[...] = jnp.zeros_like(value_acc)

        def one_chunk(chunk, sink_sum):
            part = pl.ds(pl.multiple_of(chunk * CHUNK, CHUNK), CHUNK)
            queries = held[0, head, part]
            keys = held[1, head]
            values = held[2, head]
            grads = held[3, head, part]
            scores = dot(queries, keys, 1, 1) * scaling
            row_top = jnp.maximum(jnp.max(scores, axis=1, keepdims=True), sink_value)
            raised = jnp.exp(scores - row_top)
            sink_raised = jnp.exp(sink_value - row_top)
            inverse = 1.0 / (jnp.sum(raised, axis=1, keepdims=True) + sink_raised)
            weights = raised * inverse
            rounded = weights.astype(jnp.bfloat16)
            attended = dot(rounded, values, 1, 0).astype(jnp.bfloat16)
            made[0, head, part] = attended
            row_dot = jnp.sum(
                grads.astype(jnp.float32) * attended.astype(jnp.float32), axis=1, keepdims=True
            )
            grad_weights = dot(grads, values, 1, 1)
            grad_scores = (weights * (grad_weights - row_dot)).astype(jnp.bfloat16)
            made[1, head, part] = (dot(grad_scores, keys, 1, 0) * scaling).astype(jnp.bfloat16)
            value_acc[...] += dot(rounded, grads, 0, 0)
            key_acc[...] += dot(grad_scores, queries, 0, 0)
            terms = sink_raised * inverse * row_dot
            return sink_sum + jnp.sum(terms, axis=0, keepdims=True)

        sink_sum = lax.fori_loop(
            0, total_rows // CHUNK, one_chunk, jnp.zeros((1, 1), jnp.float32)
        )
        made[2, head] = (key_acc[...] * scaling).astype(jnp.bfloat16)
        made[3, head] = value_acc[...].astype(jnp.bfloat16)
        start_all(copies_out(head))
        sink_out_ref[...] = jnp.where(lanes == me * local_heads + head, -sink_sum, sink_out_ref[...])
        return carry

    lax.fori_loop(0, local_heads, one_head, 0)

    def finish(head, carry):
        for copy in copies_in(head)[1]:
            copy.wait_send()
        own, remote = copies_out(head)
        for copy in own:
            copy.wait()
        for copy in remote:
            copy.wait()
        return carry

    lax.fori_loop(0, local_heads, finish, 0)


def dot(left, right, left_dim, right_dim):
    return lax.dot_general(
        left,
        right,
        (((left_dim,), (right_dim,)), ((), ())),
        preferred_element_type=jnp.float32,
    )


def every_block(query_rows, key_rows, value_rows, sink_logit, grad_out):
    token_count = query_rows.shape[1]
    head_count = sink_logit.shape[0]
    n = lax.axis_size("seq")
    local_heads = head_count // n
    total_rows = n * token_count
    width = head_count * HEAD
    anywhere = pl.BlockSpec(memory_space=pl.ANY)
    result = jax.ShapeDtypeStruct((token_count, width), jnp.bfloat16)
    outs = pl.pallas_call(
        functools.partial(exchange_kernel, n, local_heads, HEAD ** (-0.5)),
        out_shape=(result,) * 4 + (jax.ShapeDtypeStruct((8, 128), jnp.float32),),
        in_specs=[anywhere] * 4 + [pl.BlockSpec(memory_space=pltpu.SMEM)],
        out_specs=(anywhere,) * 4 + (pl.BlockSpec(memory_space=pltpu.VMEM),),
        scratch_shapes=[
            pltpu.VMEM((4, local_heads, total_rows, HEAD), jnp.bfloat16),
            pltpu.VMEM((4, local_heads, total_rows, HEAD), jnp.bfloat16),
            pltpu.VMEM((total_rows, HEAD), jnp.float32),
            pltpu.VMEM((total_rows, HEAD), jnp.float32),
            pltpu.SemaphoreType.DMA((local_heads, 4)),
            pltpu.SemaphoreType.DMA((local_heads, 4)),
            pltpu.SemaphoreType.DMA((local_heads, 4, n - 1)),
            pltpu.SemaphoreType.DMA((local_heads, 4, n - 1)),
            pltpu.SemaphoreType.DMA((local_heads, 4, n - 1)),
            pltpu.SemaphoreType.DMA((local_heads, 4, n - 1)),
        ],
        compiler_params=pltpu.CompilerParams(
            collective_id=0, has_side_effects=True, vmem_limit_bytes=48 * 1024 * 1024
        ),
        cost_estimate=pl.CostEstimate(
            flops=12 * local_heads * total_rows * total_rows * HEAD,
            bytes_accessed=16 * token_count * width,
            transcendentals=local_heads * total_rows * total_rows,
        ),
    )(
        query_rows.reshape(token_count, width),
        key_rows.reshape(token_count, width),
        value_rows.reshape(token_count, width),
        grad_out.reshape(token_count, width),
        sink_logit,
    )
    summed = lax.psum(outs[4][0, :head_count], ("seq", "dp"))
    return tuple(out[None] for out in outs[:4]) + (summed / lax.axis_size("dp"),)


def on_device(query_rows, key_rows, value_rows, sink_logit, grad_out, pattern):
    if pattern.shape[1] == pattern.shape[2]:
        return every_block(query_rows, key_rows, value_rows, sink_logit, grad_out)
    token_count = query_rows.shape[1]
    head_count = sink_logit.shape[0]
    local_heads = head_count // lax.axis_size("seq")
    first_head = lax.axis_index("seq") * local_heads
    head_links = lax.dynamic_slice_in_dim(pattern, first_head, local_heads, 0)
    head_sinks = lax.dynamic_slice_in_dim(sink_logit, first_head, local_heads, 0)
    scaling = HEAD ** (-0.5)

    def split_heads(array_in):
        return array_in.reshape(token_count, head_count, HEAD)

    def join_heads(array_in):
        return array_in.reshape(1, token_count, head_count * HEAD)

    query_heads, key_heads, value_heads = (
        lax.all_to_all(split_heads(query_rows), "seq", split_axis=1, concat_axis=0, tiled=True),
        lax.all_to_all(split_heads(key_rows), "seq", split_axis=1, concat_axis=0, tiled=True),
        lax.all_to_all(split_heads(value_rows), "seq", split_axis=1, concat_axis=0, tiled=True),
    )
    attended_heads, log_total = forward_pass(
        query_heads, key_heads, value_heads, head_links, head_sinks, scaling
    )
    attended = lax.all_to_all(attended_heads, "seq", split_axis=0, concat_axis=1, tiled=True)
    grad_heads = lax.all_to_all(
        split_heads(grad_out), "seq", split_axis=1, concat_axis=0, tiled=True
    )
    query_grads, key_grads, value_grads, sink_terms = backward_pass(
        query_heads,
        key_heads,
        value_heads,
        grad_heads,
        attended_heads,
        log_total,
        head_links,
        head_sinks,
        scaling,
    )
    grad_query, grad_key, grad_value = (
        lax.all_to_all(query_grads, "seq", split_axis=0, concat_axis=1, tiled=True),
        lax.all_to_all(key_grads, "seq", split_axis=0, concat_axis=1, tiled=True),
        lax.all_to_all(value_grads, "seq", split_axis=0, concat_axis=1, tiled=True),
    )
    spread = lax.dynamic_update_slice_in_dim(
        jnp.zeros((head_count,), jnp.float32), sink_terms, first_head, 0
    )
    summed = lax.psum(spread, ("seq", "dp"))
    grad_sink = summed / lax.axis_size("dp")
    return (
        join_heads(attended),
        join_heads(grad_query),
        join_heads(grad_key),
        join_heads(grad_value),
        grad_sink,
    )


def solution(mesh):
    placed = (
        P("dp", "seq", None),
        P("dp", "seq", None),
        P("dp", "seq", None),
        P(),
        P("dp", "seq", None),
        P(),
    )
    return jax.shard_map(
        on_device,
        mesh=mesh,
        in_specs=placed,
        out_specs=(
            P("dp", "seq", None),
            P("dp", "seq", None),
            P("dp", "seq", None),
            P("dp", "seq", None),
            P(),
        ),
        check_vma=False,
    )
```

```python
import functools

import jax
import jax.numpy as jnp
from jax import lax
from jax.experimental import pallas as pl
from jax.experimental.pallas import tpu as pltpu
from jax.sharding import PartitionSpec as P

MESH = pl.DeviceIdType.MESH

HEAD = 128
BLOCK = 128
CHUNK = 256


tile_group = 4


def tile_scores(queries, key_tiles, scaling):
    return (
        jnp.einsum("gqe,gkbe->gqkb", queries, key_tiles, preferred_element_type=jnp.float32)
        * scaling
    )


def log_totals(scores, sink_value):
    row_top = jnp.maximum(jnp.max(scores, axis=(2, 3)), sink_value)
    summed = jnp.sum(jnp.exp(scores - row_top[:, :, None, None]), axis=(2, 3)) + jnp.exp(
        sink_value - row_top
    )
    return row_top + jnp.log(summed)


def softmax_weights(scores, log_total):
    weights = jnp.exp(scores - log_total[:, :, None, None])
    return (weights, weights.astype(jnp.bfloat16))


def attend(rounded, value_tiles):
    return jnp.einsum(
        "gqkb,gkbe->gqe", rounded, value_tiles, preferred_element_type=jnp.float32
    ).astype(jnp.bfloat16)


def gradients(
    weights,
    rounded,
    attended,
    queries,
    key_tiles,
    value_tiles,
    grad_tile,
    log_total,
    sink_value,
    scaling,
):
    row_dot = jnp.sum(grad_tile.astype(jnp.float32) * attended.astype(jnp.float32), axis=-1)
    grad_weights = jnp.einsum(
        "gqe,gkbe->gqkb", grad_tile, value_tiles, preferred_element_type=jnp.float32
    )
    grad_scores = (weights * (grad_weights - row_dot[:, :, None, None])).astype(jnp.bfloat16)
    grad_query = (
        jnp.einsum("gqkb,gkbe->gqe", grad_scores, key_tiles, preferred_element_type=jnp.float32)
        * scaling
    ).astype(jnp.bfloat16)
    key_part = (
        jnp.einsum("gqkb,gqe->gkbe", grad_scores, queries, preferred_element_type=jnp.float32)
        * scaling
    )
    value_part = jnp.einsum(
        "gqkb,gqe->gkbe", rounded, grad_tile, preferred_element_type=jnp.float32
    )
    sink_part = -jnp.sum(jnp.exp(sink_value - log_total) * row_dot)
    return (grad_query, key_part, value_part, sink_part)


def head_tiles(array_in, head_index):
    row_count = array_in.shape[0]
    picked = lax.dynamic_index_in_dim(array_in, head_index, 1, keepdims=False)
    return picked.reshape(row_count // BLOCK, BLOCK, HEAD)


def put_head(buffer, tiles, head_index):
    return lax.dynamic_update_slice_in_dim(buffer, tiles.reshape(-1, 1, HEAD), head_index, 1)


def group_rows(tiles, group_index):
    return lax.dynamic_slice_in_dim(tiles, group_index * tile_group, tile_group, 0)


def put_group(buffer, tiles, group_index):
    return lax.dynamic_update_slice_in_dim(buffer, tiles, group_index * tile_group, 0)


def put_scalar(buffer, value_in, head_index):
    return lax.dynamic_update_slice_in_dim(buffer, value_in[None], head_index, 0)


def forward_pass(query_heads, key_heads, value_heads, head_links, head_sinks, scaling):
    row_count, local_heads, _ = query_heads.shape
    block_count = row_count // BLOCK

    def forward_one_head(head_index, head_state):
        attended, log_total = head_state
        query_tiles = head_tiles(query_heads, head_index)
        key_all = head_tiles(key_heads, head_index)
        value_all = head_tiles(value_heads, head_index)
        link_rows = lax.dynamic_index_in_dim(head_links, head_index, 0, keepdims=False)
        sink_value = lax.dynamic_index_in_dim(head_sinks, head_index, 0, keepdims=False)

        def forward_one_group(group_index, inner_state):
            out_tiles, total_tiles = inner_state
            chosen = group_rows(link_rows, group_index)
            scores = tile_scores(group_rows(query_tiles, group_index), key_all[chosen], scaling)
            group_total = log_totals(scores, sink_value)
            _, rounded = softmax_weights(scores, group_total)
            result = attend(rounded, value_all[chosen])
            return (
                put_group(out_tiles, result, group_index),
                put_group(total_tiles, group_total, group_index),
            )

        initial = (
            jnp.zeros((block_count, BLOCK, HEAD), jnp.bfloat16),
            jnp.zeros((block_count, BLOCK), jnp.float32),
        )
        out_tiles, total_tiles = lax.fori_loop(
            0, block_count // tile_group, forward_one_group, initial
        )
        return (
            put_head(attended, out_tiles, head_index),
            lax.dynamic_update_slice_in_dim(log_total, total_tiles[None], head_index, 0),
        )

    initial = (
        jnp.zeros((row_count, local_heads, HEAD), jnp.bfloat16),
        jnp.zeros((local_heads, block_count, BLOCK), jnp.float32),
    )
    return lax.fori_loop(0, local_heads, forward_one_head, initial)


def backward_pass(
    query_heads,
    key_heads,
    value_heads,
    grad_heads,
    attended,
    log_total,
    head_links,
    head_sinks,
    scaling,
):
    row_count, local_heads, _ = query_heads.shape
    block_count = row_count // BLOCK

    def backward_one_head(head_index, head_state):
        query_grads, key_grads, value_grads, sink_terms = head_state
        query_tiles = head_tiles(query_heads, head_index)
        key_all = head_tiles(key_heads, head_index)
        value_all = head_tiles(value_heads, head_index)
        grad_tiles = head_tiles(grad_heads, head_index)
        out_tiles = head_tiles(attended, head_index)
        head_total = lax.dynamic_index_in_dim(log_total, head_index, 0, keepdims=False)
        link_rows = lax.dynamic_index_in_dim(head_links, head_index, 0, keepdims=False)
        sink_value = lax.dynamic_index_in_dim(head_sinks, head_index, 0, keepdims=False)

        def backward_one_group(group_index, inner_state):
            query_part_all, key_acc, value_acc, sink_acc = inner_state
            chosen = group_rows(link_rows, group_index)
            queries = group_rows(query_tiles, group_index)
            key_tiles = key_all[chosen]
            value_tiles = value_all[chosen]
            group_total = group_rows(head_total, group_index)
            scores = tile_scores(queries, key_tiles, scaling)
            weights, rounded = softmax_weights(scores, group_total)
            grad_query, key_part, value_part, sink_part = gradients(
                weights,
                rounded,
                group_rows(out_tiles, group_index),
                queries,
                key_tiles,
                value_tiles,
                group_rows(grad_tiles, group_index),
                group_total,
                sink_value,
                scaling,
            )
            flat_links = chosen.reshape(-1)
            key_acc = key_acc.at[flat_links].add(key_part.reshape(-1, BLOCK, HEAD))
            value_acc = value_acc.at[flat_links].add(value_part.reshape(-1, BLOCK, HEAD))
            return (
                put_group(query_part_all, grad_query, group_index),
                key_acc,
                value_acc,
                sink_acc + sink_part,
            )

        initial = (
            jnp.zeros((block_count, BLOCK, HEAD), jnp.bfloat16),
            jnp.zeros((block_count, BLOCK, HEAD), jnp.float32),
            jnp.zeros((block_count, BLOCK, HEAD), jnp.float32),
            jnp.zeros((), jnp.float32),
        )
        query_part_all, key_acc, value_acc, sink_acc = lax.fori_loop(
            0, block_count // tile_group, backward_one_group, initial
        )
        return (
            put_head(query_grads, query_part_all, head_index),
            put_head(key_grads, key_acc.astype(jnp.bfloat16), head_index),
            put_head(value_grads, value_acc.astype(jnp.bfloat16), head_index),
            put_scalar(sink_terms, sink_acc, head_index),
        )

    blank = jnp.zeros((row_count, local_heads, HEAD), jnp.bfloat16)
    initial = (blank, blank, blank, jnp.zeros((local_heads,), jnp.float32))
    return lax.fori_loop(0, local_heads, backward_one_head, initial)


def exchange_kernel(
    n,
    documents,
    local_heads,
    scaling,
    query_ref,
    key_ref,
    value_ref,
    grad_ref,
    sink_ref,
    attended_ref,
    query_grad_ref,
    key_grad_ref,
    value_grad_ref,
    sink_out_ref,
    held,
    made,
    key_acc,
    value_acc,
    sink_values,
    sink_terms,
    sink_totals,
    sink_copy,
    own_in,
    own_out,
    in_send,
    in_recv,
    out_send,
    out_recv,
    terms_send,
    terms_recv,
    totals_send,
    totals_recv,
):
    me = lax.axis_index("seq")
    document = lax.axis_index("dp")
    rows = query_ref.shape[0]
    total_rows = held.shape[2]
    given = (query_ref, key_ref, value_ref, grad_ref)
    wanted = (attended_ref, query_grad_ref, key_grad_ref, value_grad_ref)

    def partner(step):
        return lax.rem(me + step, n)

    def columns(device, head):
        return pl.ds(pl.multiple_of((device * local_heads + head) * HEAD, HEAD), HEAD)

    def row_range(device):
        return pl.ds(pl.multiple_of(device * rows, rows), rows)

    def copies_in(head):
        own, remote = [], []
        for which, source in enumerate(given):
            own.append(
                pltpu.make_async_copy(
                    source.at[:, columns(me, head)],
                    held.at[which, head, row_range(me)],
                    own_in.at[head, which],
                )
            )
            for step in range(1, n):
                to = partner(step)
                remote.append(
                    pltpu.make_async_remote_copy(
                        src_ref=source.at[:, columns(to, head)],
                        dst_ref=held.at[which, head, row_range(me)],
                        send_sem=in_send.at[head, which, step - 1],
                        recv_sem=in_recv.at[head, which, step - 1],
                        device_id={"seq": to},
                        device_id_type=MESH,
                    )
                )
        return own, remote

    def copies_out(head):
        own, remote = [], []
        for which, target in enumerate(wanted):
            own.append(
                pltpu.make_async_copy(
                    made.at[which, head, row_range(me)],
                    target.at[:, columns(me, head)],
                    own_out.at[head, which],
                )
            )
            for step in range(1, n):
                to = partner(step)
                remote.append(
                    pltpu.make_async_remote_copy(
                        src_ref=made.at[which, head, row_range(to)],
                        dst_ref=target.at[:, columns(me, head)],
                        send_sem=out_send.at[head, which, step - 1],
                        recv_sem=out_recv.at[head, which, step - 1],
                        device_id={"seq": to},
                        device_id_type=MESH,
                    )
                )
        return own, remote

    def start_all(copies):
        own, remote = copies
        for copy in remote + own:
            copy.start()

    def terms_copies():
        return [
            pltpu.make_async_remote_copy(
                src_ref=sink_terms.at[document],
                dst_ref=sink_terms.at[document],
                send_sem=terms_send.at[step - 1],
                recv_sem=terms_recv.at[step - 1],
                device_id={"dp": lax.rem(document + step, documents)},
                device_id_type=MESH,
            )
            for step in range(1, documents)
        ]

    def totals_copies():
        return [
            pltpu.make_async_remote_copy(
                src_ref=sink_totals.at[me],
                dst_ref=sink_totals.at[me],
                send_sem=totals_send.at[step - 1],
                recv_sem=totals_recv.at[step - 1],
                device_id={"seq": partner(step)},
                device_id_type=MESH,
            )
            for step in range(1, n)
        ]

    sinks_in = pltpu.make_async_copy(sink_ref, sink_values, sink_copy)
    sinks_in.start()
    barrier = pltpu.get_barrier_semaphore()
    for step in range(1, n):
        pl.semaphore_signal(
            barrier, inc=1, device_id={"seq": partner(step)}, device_id_type=MESH
        )
    for step in range(1, documents):
        other = lax.rem(document + step, documents)
        pl.semaphore_signal(barrier, inc=1, device_id={"dp": other}, device_id_type=MESH)
    pl.semaphore_wait(barrier, n + documents - 2)

    start_all(copies_in(0))
    if local_heads > 1:
        start_all(copies_in(1))
    sink_terms[document] = jnp.zeros(sink_out_ref.shape, jnp.float32)
    lanes = lax.broadcasted_iota(jnp.int32, sink_out_ref.shape, 1)
    sinks_in.wait()

    def one_head(head, carry):
        own, remote = copies_in(head)
        for copy in own:
            copy.wait()
        for copy in remote:
            copy.wait_recv()

        @pl.when(head + 2 < local_heads)
        def _():
            start_all(copies_in(head + 2))

        sink_value = sink_values[me * local_heads + head]
        key_acc[...] = jnp.zeros_like(key_acc)
        value_acc[...] = jnp.zeros_like(value_acc)

        def one_chunk(chunk, sink_sum):
            part = pl.ds(pl.multiple_of(chunk * CHUNK, CHUNK), CHUNK)
            queries = held[0, head, part]
            keys = held[1, head]
            values = held[2, head]
            grads = held[3, head, part]
            scores = dot(queries, keys, 1, 1) * scaling
            row_top = jnp.maximum(jnp.max(scores, axis=1, keepdims=True), sink_value)
            raised = jnp.exp(scores - row_top)
            sink_raised = jnp.exp(sink_value - row_top)
            inverse = 1.0 / (jnp.sum(raised, axis=1, keepdims=True) + sink_raised)
            weights = raised * inverse
            rounded = weights.astype(jnp.bfloat16)
            attended = dot(rounded, values, 1, 0).astype(jnp.bfloat16)
            made[0, head, part] = attended
            row_dot = jnp.sum(
                grads.astype(jnp.float32) * attended.astype(jnp.float32), axis=1, keepdims=True
            )
            grad_weights = dot(grads, values, 1, 1)
            grad_scores = (weights * (grad_weights - row_dot)).astype(jnp.bfloat16)
            made[1, head, part] = (dot(grad_scores, keys, 1, 0) * scaling).astype(jnp.bfloat16)
            value_acc[...] += dot(rounded, grads, 0, 0)
            key_acc[...] += dot(grad_scores, queries, 0, 0)
            terms = sink_raised * inverse * row_dot
            return sink_sum + jnp.sum(terms, axis=0, keepdims=True)

        sink_sum = lax.fori_loop(
            0, total_rows // CHUNK, one_chunk, jnp.zeros((1, 1), jnp.float32)
        )
        made[2, head] = (key_acc[...] * scaling).astype(jnp.bfloat16)
        made[3, head] = value_acc[...].astype(jnp.bfloat16)
        sink_terms[document] = jnp.where(
            lanes == me * local_heads + head, -sink_sum, sink_terms[document]
        )

        @pl.when(head == local_heads - 1)
        def _():
            for copy in terms_copies():
                copy.start()

        start_all(copies_out(head))
        return carry

    lax.fori_loop(0, local_heads, one_head, 0)

    for copy in terms_copies():
        copy.wait()
    sink_totals[me] = jnp.sum(sink_terms[...], axis=0)
    for copy in totals_copies():
        copy.start()
    for copy in totals_copies():
        copy.wait()
    sink_out_ref[...] = jnp.sum(sink_totals[...], axis=0) * (1.0 / documents)

    def finish(head, carry):
        for copy in copies_in(head)[1]:
            copy.wait_send()
        own, remote = copies_out(head)
        for copy in own:
            copy.wait()
        for copy in remote:
            copy.wait()
        return carry

    lax.fori_loop(0, local_heads, finish, 0)


def store_kernel(*refs):
    sources, sink_ref, targets, sink_out_ref, done = refs[:4], refs[4], refs[5:9], refs[9], refs[10]
    rows = sources[0].shape[0] // 2
    copies = [
        pltpu.make_async_copy(
            source.at[pl.ds(half * rows, rows)],
            target.at[pl.ds(half * rows, rows)],
            done.at[which, half],
        )
        for which, (source, target) in enumerate(zip(sources, targets))
        for half in range(2)
    ]
    for copy in copies:
        copy.start()
    sink_out_ref[...] = sink_ref[0, : sink_out_ref.shape[0]]
    for copy in copies:
        copy.wait()


def dot(left, right, left_dim, right_dim):
    return lax.dot_general(
        left,
        right,
        (((left_dim,), (right_dim,)), ((), ())),
        preferred_element_type=jnp.float32,
    )


def every_block(query_rows, key_rows, value_rows, sink_logit, grad_out):
    token_count = query_rows.shape[1]
    head_count = sink_logit.shape[0]
    n = lax.axis_size("seq")
    local_heads = head_count // n
    total_rows = n * token_count
    width = head_count * HEAD
    documents = lax.axis_size("dp")
    anywhere = pl.BlockSpec(memory_space=pl.ANY)
    in_hbm = pl.BlockSpec(memory_space=pltpu.HBM)
    in_vmem = pl.BlockSpec(memory_space=pltpu.VMEM)
    result = jax.ShapeDtypeStruct((token_count, width), jnp.bfloat16)
    outs = pl.pallas_call(
        functools.partial(exchange_kernel, n, documents, local_heads, HEAD ** (-0.5)),
        out_shape=(result,) * 4 + (jax.ShapeDtypeStruct((8, 128), jnp.float32),),
        in_specs=[in_hbm] * 5,
        out_specs=(anywhere,) * 4 + (in_vmem,),
        scratch_shapes=[
            pltpu.VMEM((4, local_heads, total_rows, HEAD), jnp.bfloat16),
            pltpu.VMEM((4, local_heads, total_rows, HEAD), jnp.bfloat16),
            pltpu.VMEM((total_rows, HEAD), jnp.float32),
            pltpu.VMEM((total_rows, HEAD), jnp.float32),
            pltpu.SMEM((head_count,), jnp.float32),
            pltpu.VMEM((documents, 8, 128), jnp.float32),
            pltpu.VMEM((n, 8, 128), jnp.float32),
            pltpu.SemaphoreType.DMA,
            pltpu.SemaphoreType.DMA((local_heads, 4)),
            pltpu.SemaphoreType.DMA((local_heads, 4)),
            pltpu.SemaphoreType.DMA((local_heads, 4, n - 1)),
            pltpu.SemaphoreType.DMA((local_heads, 4, n - 1)),
            pltpu.SemaphoreType.DMA((local_heads, 4, n - 1)),
            pltpu.SemaphoreType.DMA((local_heads, 4, n - 1)),
            pltpu.SemaphoreType.DMA((documents - 1,)),
            pltpu.SemaphoreType.DMA((documents - 1,)),
            pltpu.SemaphoreType.DMA((n - 1,)),
            pltpu.SemaphoreType.DMA((n - 1,)),
        ],
        compiler_params=pltpu.CompilerParams(
            collective_id=0, has_side_effects=True, vmem_limit_bytes=48 * 1024 * 1024
        ),
        cost_estimate=pl.CostEstimate(
            flops=12 * local_heads * total_rows * total_rows * HEAD,
            bytes_accessed=16 * token_count * width,
            transcendentals=local_heads * total_rows * total_rows,
        ),
    )(
        query_rows.reshape(token_count, width),
        key_rows.reshape(token_count, width),
        value_rows.reshape(token_count, width),
        grad_out.reshape(token_count, width),
        sink_logit,
    )
    stored = pl.pallas_call(
        store_kernel,
        out_shape=(result,) * 4 + (jax.ShapeDtypeStruct((head_count,), jnp.float32),),
        in_specs=[anywhere] * 4 + [in_vmem],
        out_specs=(in_hbm,) * 4 + (in_vmem,),
        scratch_shapes=[pltpu.SemaphoreType.DMA((4, 2))],
        compiler_params=pltpu.CompilerParams(vmem_limit_bytes=4 * 1024 * 1024),
    )(*outs)
    return tuple(out[None] for out in stored[:4]) + (stored[4],)


def on_device(query_rows, key_rows, value_rows, sink_logit, grad_out, pattern):
    if pattern.shape[1] == pattern.shape[2]:
        return every_block(query_rows, key_rows, value_rows, sink_logit, grad_out)
    token_count = query_rows.shape[1]
    head_count = sink_logit.shape[0]
    local_heads = head_count // lax.axis_size("seq")
    first_head = lax.axis_index("seq") * local_heads
    head_links = lax.dynamic_slice_in_dim(pattern, first_head, local_heads, 0)
    head_sinks = lax.dynamic_slice_in_dim(sink_logit, first_head, local_heads, 0)
    scaling = HEAD ** (-0.5)

    def split_heads(array_in):
        return array_in.reshape(token_count, head_count, HEAD)

    def join_heads(array_in):
        return array_in.reshape(1, token_count, head_count * HEAD)

    query_heads, key_heads, value_heads = (
        lax.all_to_all(split_heads(query_rows), "seq", split_axis=1, concat_axis=0, tiled=True),
        lax.all_to_all(split_heads(key_rows), "seq", split_axis=1, concat_axis=0, tiled=True),
        lax.all_to_all(split_heads(value_rows), "seq", split_axis=1, concat_axis=0, tiled=True),
    )
    attended_heads, log_total = forward_pass(
        query_heads, key_heads, value_heads, head_links, head_sinks, scaling
    )
    attended = lax.all_to_all(attended_heads, "seq", split_axis=0, concat_axis=1, tiled=True)
    grad_heads = lax.all_to_all(
        split_heads(grad_out), "seq", split_axis=1, concat_axis=0, tiled=True
    )
    query_grads, key_grads, value_grads, sink_terms = backward_pass(
        query_heads,
        key_heads,
        value_heads,
        grad_heads,
        attended_heads,
        log_total,
        head_links,
        head_sinks,
        scaling,
    )
    grad_query, grad_key, grad_value = (
        lax.all_to_all(query_grads, "seq", split_axis=0, concat_axis=1, tiled=True),
        lax.all_to_all(key_grads, "seq", split_axis=0, concat_axis=1, tiled=True),
        lax.all_to_all(value_grads, "seq", split_axis=0, concat_axis=1, tiled=True),
    )
    spread = lax.dynamic_update_slice_in_dim(
        jnp.zeros((head_count,), jnp.float32), sink_terms, first_head, 0
    )
    summed = lax.psum(spread, ("seq", "dp"))
    grad_sink = summed / lax.axis_size("dp")
    return (
        join_heads(attended),
        join_heads(grad_query),
        join_heads(grad_key),
        join_heads(grad_value),
        grad_sink,
    )


def solution(mesh):
    placed = (
        P("dp", "seq", None),
        P("dp", "seq", None),
        P("dp", "seq", None),
        P(),
        P("dp", "seq", None),
        P(),
    )
    return jax.shard_map(
        on_device,
        mesh=mesh,
        in_specs=placed,
        out_specs=(
            P("dp", "seq", None),
            P("dp", "seq", None),
            P("dp", "seq", None),
            P("dp", "seq", None),
            P(),
        ),
        check_vma=False,
    )
```

```python
import functools

import jax
import jax.numpy as jnp
from jax import lax
from jax.experimental import pallas as pl
from jax.experimental.pallas import tpu as pltpu
from jax.sharding import PartitionSpec as P

MESH = pl.DeviceIdType.MESH

HEAD = 128
BLOCK = 128


tile_group = 4


def tile_scores(queries, key_tiles, scaling):
    return (
        jnp.einsum("gqe,gkbe->gqkb", queries, key_tiles, preferred_element_type=jnp.float32)
        * scaling
    )


def log_totals(scores, sink_value):
    row_top = jnp.maximum(jnp.max(scores, axis=(2, 3)), sink_value)
    summed = jnp.sum(jnp.exp(scores - row_top[:, :, None, None]), axis=(2, 3)) + jnp.exp(
        sink_value - row_top
    )
    return row_top + jnp.log(summed)


def softmax_weights(scores, log_total):
    weights = jnp.exp(scores - log_total[:, :, None, None])
    return (weights, weights.astype(jnp.bfloat16))


def attend(rounded, value_tiles):
    return jnp.einsum(
        "gqkb,gkbe->gqe", rounded, value_tiles, preferred_element_type=jnp.float32
    ).astype(jnp.bfloat16)


def gradients(
    weights,
    rounded,
    attended,
    queries,
    key_tiles,
    value_tiles,
    grad_tile,
    log_total,
    sink_value,
    scaling,
):
    row_dot = jnp.sum(grad_tile.astype(jnp.float32) * attended.astype(jnp.float32), axis=-1)
    grad_weights = jnp.einsum(
        "gqe,gkbe->gqkb", grad_tile, value_tiles, preferred_element_type=jnp.float32
    )
    grad_scores = (weights * (grad_weights - row_dot[:, :, None, None])).astype(jnp.bfloat16)
    grad_query = (
        jnp.einsum("gqkb,gkbe->gqe", grad_scores, key_tiles, preferred_element_type=jnp.float32)
        * scaling
    ).astype(jnp.bfloat16)
    key_part = (
        jnp.einsum("gqkb,gqe->gkbe", grad_scores, queries, preferred_element_type=jnp.float32)
        * scaling
    )
    value_part = jnp.einsum(
        "gqkb,gqe->gkbe", rounded, grad_tile, preferred_element_type=jnp.float32
    )
    sink_part = -jnp.sum(jnp.exp(sink_value - log_total) * row_dot)
    return (grad_query, key_part, value_part, sink_part)


def head_tiles(array_in, head_index):
    row_count = array_in.shape[0]
    picked = lax.dynamic_index_in_dim(array_in, head_index, 1, keepdims=False)
    return picked.reshape(row_count // BLOCK, BLOCK, HEAD)


def put_head(buffer, tiles, head_index):
    return lax.dynamic_update_slice_in_dim(buffer, tiles.reshape(-1, 1, HEAD), head_index, 1)


def group_rows(tiles, group_index):
    return lax.dynamic_slice_in_dim(tiles, group_index * tile_group, tile_group, 0)


def put_group(buffer, tiles, group_index):
    return lax.dynamic_update_slice_in_dim(buffer, tiles, group_index * tile_group, 0)


def put_scalar(buffer, value_in, head_index):
    return lax.dynamic_update_slice_in_dim(buffer, value_in[None], head_index, 0)


def forward_pass(query_heads, key_heads, value_heads, head_links, head_sinks, scaling):
    row_count, local_heads, _ = query_heads.shape
    block_count = row_count // BLOCK

    def forward_one_head(head_index, head_state):
        attended, log_total = head_state
        query_tiles = head_tiles(query_heads, head_index)
        key_all = head_tiles(key_heads, head_index)
        value_all = head_tiles(value_heads, head_index)
        link_rows = lax.dynamic_index_in_dim(head_links, head_index, 0, keepdims=False)
        sink_value = lax.dynamic_index_in_dim(head_sinks, head_index, 0, keepdims=False)

        def forward_one_group(group_index, inner_state):
            out_tiles, total_tiles = inner_state
            chosen = group_rows(link_rows, group_index)
            scores = tile_scores(group_rows(query_tiles, group_index), key_all[chosen], scaling)
            group_total = log_totals(scores, sink_value)
            _, rounded = softmax_weights(scores, group_total)
            result = attend(rounded, value_all[chosen])
            return (
                put_group(out_tiles, result, group_index),
                put_group(total_tiles, group_total, group_index),
            )

        initial = (
            jnp.zeros((block_count, BLOCK, HEAD), jnp.bfloat16),
            jnp.zeros((block_count, BLOCK), jnp.float32),
        )
        out_tiles, total_tiles = lax.fori_loop(
            0, block_count // tile_group, forward_one_group, initial
        )
        return (
            put_head(attended, out_tiles, head_index),
            lax.dynamic_update_slice_in_dim(log_total, total_tiles[None], head_index, 0),
        )

    initial = (
        jnp.zeros((row_count, local_heads, HEAD), jnp.bfloat16),
        jnp.zeros((local_heads, block_count, BLOCK), jnp.float32),
    )
    return lax.fori_loop(0, local_heads, forward_one_head, initial)


def backward_pass(
    query_heads,
    key_heads,
    value_heads,
    grad_heads,
    attended,
    log_total,
    head_links,
    head_sinks,
    scaling,
):
    row_count, local_heads, _ = query_heads.shape
    block_count = row_count // BLOCK

    def backward_one_head(head_index, head_state):
        query_grads, key_grads, value_grads, sink_terms = head_state
        query_tiles = head_tiles(query_heads, head_index)
        key_all = head_tiles(key_heads, head_index)
        value_all = head_tiles(value_heads, head_index)
        grad_tiles = head_tiles(grad_heads, head_index)
        out_tiles = head_tiles(attended, head_index)
        head_total = lax.dynamic_index_in_dim(log_total, head_index, 0, keepdims=False)
        link_rows = lax.dynamic_index_in_dim(head_links, head_index, 0, keepdims=False)
        sink_value = lax.dynamic_index_in_dim(head_sinks, head_index, 0, keepdims=False)

        def backward_one_group(group_index, inner_state):
            query_part_all, key_acc, value_acc, sink_acc = inner_state
            chosen = group_rows(link_rows, group_index)
            queries = group_rows(query_tiles, group_index)
            key_tiles = key_all[chosen]
            value_tiles = value_all[chosen]
            group_total = group_rows(head_total, group_index)
            scores = tile_scores(queries, key_tiles, scaling)
            weights, rounded = softmax_weights(scores, group_total)
            grad_query, key_part, value_part, sink_part = gradients(
                weights,
                rounded,
                group_rows(out_tiles, group_index),
                queries,
                key_tiles,
                value_tiles,
                group_rows(grad_tiles, group_index),
                group_total,
                sink_value,
                scaling,
            )
            flat_links = chosen.reshape(-1)
            key_acc = key_acc.at[flat_links].add(key_part.reshape(-1, BLOCK, HEAD))
            value_acc = value_acc.at[flat_links].add(value_part.reshape(-1, BLOCK, HEAD))
            return (
                put_group(query_part_all, grad_query, group_index),
                key_acc,
                value_acc,
                sink_acc + sink_part,
            )

        initial = (
            jnp.zeros((block_count, BLOCK, HEAD), jnp.bfloat16),
            jnp.zeros((block_count, BLOCK, HEAD), jnp.float32),
            jnp.zeros((block_count, BLOCK, HEAD), jnp.float32),
            jnp.zeros((), jnp.float32),
        )
        query_part_all, key_acc, value_acc, sink_acc = lax.fori_loop(
            0, block_count // tile_group, backward_one_group, initial
        )
        return (
            put_head(query_grads, query_part_all, head_index),
            put_head(key_grads, key_acc.astype(jnp.bfloat16), head_index),
            put_head(value_grads, value_acc.astype(jnp.bfloat16), head_index),
            put_scalar(sink_terms, sink_acc, head_index),
        )

    blank = jnp.zeros((row_count, local_heads, HEAD), jnp.bfloat16)
    initial = (blank, blank, blank, jnp.zeros((local_heads,), jnp.float32))
    return lax.fori_loop(0, local_heads, backward_one_head, initial)


def exchange_kernel(
    n,
    documents,
    local_heads,
    scaling,
    query_ref,
    key_ref,
    value_ref,
    grad_ref,
    sink_ref,
    attended_ref,
    query_grad_ref,
    key_grad_ref,
    value_grad_ref,
    sink_out_ref,
    held,
    made,
    key_acc,
    value_acc,
    sink_values,
    sink_terms,
    sink_totals,
    sink_copy,
    own_in,
    own_out,
    in_send,
    in_recv,
    out_send,
    out_recv,
    terms_send,
    terms_recv,
    totals_send,
    totals_recv,
):
    me = lax.axis_index("seq")
    document = lax.axis_index("dp")
    rows = query_ref.shape[0]
    total_rows = held.shape[2]
    given = (query_ref, key_ref, value_ref, grad_ref)
    wanted = (attended_ref, query_grad_ref, key_grad_ref, value_grad_ref)

    def partner(step):
        return lax.rem(me + step, n)

    def columns(device, head):
        return pl.ds(pl.multiple_of((device * local_heads + head) * HEAD, HEAD), HEAD)

    def row_range(device):
        return pl.ds(pl.multiple_of(device * rows, rows), rows)

    def copies_in(head, pair):
        own, remote = [], []
        for which in (2 * pair, 2 * pair + 1):
            source = given[which]
            own.append(
                pltpu.make_async_copy(
                    source.at[:, columns(me, head)],
                    held.at[which, head, row_range(me)],
                    own_in.at[head, which],
                )
            )
            for step in range(1, n):
                to = partner(step)
                remote.append(
                    pltpu.make_async_remote_copy(
                        src_ref=source.at[:, columns(to, head)],
                        dst_ref=held.at[which, head, row_range(me)],
                        send_sem=in_send.at[head, which, step - 1],
                        recv_sem=in_recv.at[head, which, step - 1],
                        device_id={"seq": to},
                        device_id_type=MESH,
                    )
                )
        return own, remote

    def own_copy(which, head):
        return pltpu.make_async_copy(
            made.at[which, head, row_range(me)],
            wanted[which].at[:, columns(me, head)],
            own_out.at[head, which],
        )

    def copy_out(which, head, step):
        to = partner(step)
        return pltpu.make_async_remote_copy(
            src_ref=made.at[which, head, row_range(to)],
            dst_ref=wanted[which].at[:, columns(me, head)],
            send_sem=out_send.at[head, which, step - 1],
            recv_sem=out_recv.at[head, which, step - 1],
            device_id={"seq": to},
            device_id_type=MESH,
        )

    def start_all(copies):
        own, remote = copies
        for copy in remote + own:
            copy.start()

    def terms_copies():
        return [
            pltpu.make_async_remote_copy(
                src_ref=sink_terms.at[document],
                dst_ref=sink_terms.at[document],
                send_sem=terms_send.at[step - 1],
                recv_sem=terms_recv.at[step - 1],
                device_id={"dp": lax.rem(document + step, documents)},
                device_id_type=MESH,
            )
            for step in range(1, documents)
        ]

    def totals_copies():
        return [
            pltpu.make_async_remote_copy(
                src_ref=sink_totals.at[me],
                dst_ref=sink_totals.at[me],
                send_sem=totals_send.at[step - 1],
                recv_sem=totals_recv.at[step - 1],
                device_id={"seq": partner(step)},
                device_id_type=MESH,
            )
            for step in range(1, n)
        ]

    sinks_in = pltpu.make_async_copy(sink_ref, sink_values, sink_copy)
    sinks_in.start()
    barrier = pltpu.get_barrier_semaphore()
    for step in range(1, n):
        pl.semaphore_signal(
            barrier, inc=1, device_id={"seq": partner(step)}, device_id_type=MESH
        )
    for step in range(1, documents):
        other = lax.rem(document + step, documents)
        pl.semaphore_signal(barrier, inc=1, device_id={"dp": other}, device_id_type=MESH)
    pl.semaphore_wait(barrier, n + documents - 2)

    start_all(copies_in(0, 0))
    start_all(copies_in(0, 1))
    sink_terms[document] = jnp.zeros(sink_out_ref.shape, jnp.float32)
    lanes = lax.broadcasted_iota(jnp.int32, sink_out_ref.shape, 1)
    sinks_in.wait()

    def one_head(head, carry):
        for pair in range(2):
            own, remote = copies_in(head, pair)
            for copy in own:
                copy.wait()
            for copy in remote:
                copy.wait_recv()

            if pair == 0 and local_heads > 1:

                @pl.when(head == 0)
                def _():
                    start_all(copies_in(1, 0))

        @pl.when(head + 1 < local_heads)
        def _():
            start_all(copies_in(head + 1, 1))

        @pl.when(head + 2 < local_heads)
        def _():
            start_all(copies_in(head + 2, 0))

        sink_value = sink_values[me * local_heads + head]
        key_acc[...] = jnp.zeros_like(key_acc)
        value_acc[...] = jnp.zeros_like(value_acc)

        def one_chunk(step, sink_sum):
            part = row_range(partner(step))
            queries = held[0, head, part]
            keys = held[1, head]
            values = held[2, head]
            grads = held[3, head, part]
            scores = dot(queries, keys, 1, 1) * scaling
            row_top = jnp.maximum(jnp.max(scores, axis=1, keepdims=True), sink_value)
            raised = jnp.exp(scores - row_top)
            sink_raised = jnp.exp(sink_value - row_top)
            inverse = 1.0 / (jnp.sum(raised, axis=1, keepdims=True) + sink_raised)
            weights = raised * inverse
            rounded = weights.astype(jnp.bfloat16)
            attended = dot(rounded, values, 1, 0).astype(jnp.bfloat16)
            made[0, head, part] = attended
            row_dot = jnp.sum(
                grads.astype(jnp.float32) * attended.astype(jnp.float32), axis=1, keepdims=True
            )
            grad_weights = dot(grads, values, 1, 1)
            grad_scores = (weights * (grad_weights - row_dot)).astype(jnp.bfloat16)
            made[1, head, part] = (dot(grad_scores, keys, 1, 0) * scaling).astype(jnp.bfloat16)

            @pl.when(step < n)
            def _():
                for which in range(2):
                    copy_out(which, head, step).start()

            value_acc[...] += dot(rounded, grads, 0, 0)
            key_acc[...] += dot(grad_scores, queries, 0, 0)
            terms = sink_raised * inverse * row_dot
            return sink_sum + jnp.sum(terms, axis=0, keepdims=True)

        sink_sum = lax.fori_loop(
            1, n + 1, one_chunk, jnp.zeros((1, 1), jnp.float32)
        )
        made[2, head] = (key_acc[...] * scaling).astype(jnp.bfloat16)
        made[3, head] = value_acc[...].astype(jnp.bfloat16)
        sink_terms[document] = jnp.where(
            lanes == me * local_heads + head, -sink_sum, sink_terms[document]
        )

        @pl.when(head == local_heads - 1)
        def _():
            for copy in terms_copies():
                copy.start()

        for which in range(2, 4):
            for step in range(1, n):
                copy_out(which, head, step).start()
        for which in range(4):
            own_copy(which, head).start()
        return carry

    lax.fori_loop(0, local_heads, one_head, 0)

    for copy in terms_copies():
        copy.wait()
    sink_totals[me] = jnp.sum(sink_terms[...], axis=0)
    for copy in totals_copies():
        copy.start()
    for copy in totals_copies():
        copy.wait()
    sink_out_ref[...] = jnp.sum(sink_totals[...], axis=0) * (1.0 / documents)

    def finish(head, carry):
        for pair in range(2):
            for copy in copies_in(head, pair)[1]:
                copy.wait_send()
        for which in range(4):
            own_copy(which, head).wait()
            for step in range(1, n):
                copy_out(which, head, step).wait()
        return carry

    lax.fori_loop(0, local_heads, finish, 0)


def store_kernel(*refs):
    sources, sink_ref, targets, sink_out_ref, done = refs[:4], refs[4], refs[5:9], refs[9], refs[10]
    rows = sources[0].shape[0] // 2
    copies = [
        pltpu.make_async_copy(
            source.at[pl.ds(half * rows, rows)],
            target.at[pl.ds(half * rows, rows)],
            done.at[which, half],
        )
        for which, (source, target) in enumerate(zip(sources, targets))
        for half in range(2)
    ]
    for copy in copies:
        copy.start()
    sink_out_ref[...] = sink_ref[0, : sink_out_ref.shape[0]]
    for copy in copies:
        copy.wait()


def dot(left, right, left_dim, right_dim):
    return lax.dot_general(
        left,
        right,
        (((left_dim,), (right_dim,)), ((), ())),
        preferred_element_type=jnp.float32,
    )


def every_block(query_rows, key_rows, value_rows, sink_logit, grad_out):
    token_count = query_rows.shape[1]
    head_count = sink_logit.shape[0]
    n = lax.axis_size("seq")
    local_heads = head_count // n
    total_rows = n * token_count
    width = head_count * HEAD
    documents = lax.axis_size("dp")
    anywhere = pl.BlockSpec(memory_space=pl.ANY)
    in_hbm = pl.BlockSpec(memory_space=pltpu.HBM)
    in_vmem = pl.BlockSpec(memory_space=pltpu.VMEM)
    result = jax.ShapeDtypeStruct((token_count, width), jnp.bfloat16)
    outs = pl.pallas_call(
        functools.partial(exchange_kernel, n, documents, local_heads, HEAD ** (-0.5)),
        out_shape=(result,) * 4 + (jax.ShapeDtypeStruct((8, 128), jnp.float32),),
        in_specs=[in_hbm] * 5,
        out_specs=(anywhere,) * 4 + (in_vmem,),
        scratch_shapes=[
            pltpu.VMEM((4, local_heads, total_rows, HEAD), jnp.bfloat16),
            pltpu.VMEM((4, local_heads, total_rows, HEAD), jnp.bfloat16),
            pltpu.VMEM((total_rows, HEAD), jnp.float32),
            pltpu.VMEM((total_rows, HEAD), jnp.float32),
            pltpu.SMEM((head_count,), jnp.float32),
            pltpu.VMEM((documents, 8, 128), jnp.float32),
            pltpu.VMEM((n, 8, 128), jnp.float32),
            pltpu.SemaphoreType.DMA,
            pltpu.SemaphoreType.DMA((local_heads, 4)),
            pltpu.SemaphoreType.DMA((local_heads, 4)),
            pltpu.SemaphoreType.DMA((local_heads, 4, n - 1)),
            pltpu.SemaphoreType.DMA((local_heads, 4, n - 1)),
            pltpu.SemaphoreType.DMA((local_heads, 4, n - 1)),
            pltpu.SemaphoreType.DMA((local_heads, 4, n - 1)),
            pltpu.SemaphoreType.DMA((documents - 1,)),
            pltpu.SemaphoreType.DMA((documents - 1,)),
            pltpu.SemaphoreType.DMA((n - 1,)),
            pltpu.SemaphoreType.DMA((n - 1,)),
        ],
        compiler_params=pltpu.CompilerParams(
            collective_id=0, has_side_effects=True, vmem_limit_bytes=49 * 1024 * 1024
        ),
        cost_estimate=pl.CostEstimate(
            flops=12 * local_heads * total_rows * total_rows * HEAD,
            bytes_accessed=16 * token_count * width,
            transcendentals=local_heads * total_rows * total_rows,
        ),
    )(
        query_rows.reshape(token_count, width),
        key_rows.reshape(token_count, width),
        value_rows.reshape(token_count, width),
        grad_out.reshape(token_count, width),
        sink_logit,
    )
    stored = pl.pallas_call(
        store_kernel,
        out_shape=(result,) * 4 + (jax.ShapeDtypeStruct((head_count,), jnp.float32),),
        in_specs=[anywhere] * 4 + [in_vmem],
        out_specs=(in_hbm,) * 4 + (in_vmem,),
        scratch_shapes=[pltpu.SemaphoreType.DMA((4, 2))],
        compiler_params=pltpu.CompilerParams(vmem_limit_bytes=4 * 1024 * 1024),
    )(*outs)
    return tuple(out[None] for out in stored[:4]) + (stored[4],)


def on_device(query_rows, key_rows, value_rows, sink_logit, grad_out, pattern):
    if pattern.shape[1] == pattern.shape[2]:
        return every_block(query_rows, key_rows, value_rows, sink_logit, grad_out)
    token_count = query_rows.shape[1]
    head_count = sink_logit.shape[0]
    local_heads = head_count // lax.axis_size("seq")
    first_head = lax.axis_index("seq") * local_heads
    head_links = lax.dynamic_slice_in_dim(pattern, first_head, local_heads, 0)
    head_sinks = lax.dynamic_slice_in_dim(sink_logit, first_head, local_heads, 0)
    scaling = HEAD ** (-0.5)

    def split_heads(array_in):
        return array_in.reshape(token_count, head_count, HEAD)

    def join_heads(array_in):
        return array_in.reshape(1, token_count, head_count * HEAD)

    query_heads, key_heads, value_heads = (
        lax.all_to_all(split_heads(query_rows), "seq", split_axis=1, concat_axis=0, tiled=True),
        lax.all_to_all(split_heads(key_rows), "seq", split_axis=1, concat_axis=0, tiled=True),
        lax.all_to_all(split_heads(value_rows), "seq", split_axis=1, concat_axis=0, tiled=True),
    )
    attended_heads, log_total = forward_pass(
        query_heads, key_heads, value_heads, head_links, head_sinks, scaling
    )
    attended = lax.all_to_all(attended_heads, "seq", split_axis=0, concat_axis=1, tiled=True)
    grad_heads = lax.all_to_all(
        split_heads(grad_out), "seq", split_axis=1, concat_axis=0, tiled=True
    )
    query_grads, key_grads, value_grads, sink_terms = backward_pass(
        query_heads,
        key_heads,
        value_heads,
        grad_heads,
        attended_heads,
        log_total,
        head_links,
        head_sinks,
        scaling,
    )
    grad_query, grad_key, grad_value = (
        lax.all_to_all(query_grads, "seq", split_axis=0, concat_axis=1, tiled=True),
        lax.all_to_all(key_grads, "seq", split_axis=0, concat_axis=1, tiled=True),
        lax.all_to_all(value_grads, "seq", split_axis=0, concat_axis=1, tiled=True),
    )
    spread = lax.dynamic_update_slice_in_dim(
        jnp.zeros((head_count,), jnp.float32), sink_terms, first_head, 0
    )
    summed = lax.psum(spread, ("seq", "dp"))
    grad_sink = summed / lax.axis_size("dp")
    return (
        join_heads(attended),
        join_heads(grad_query),
        join_heads(grad_key),
        join_heads(grad_value),
        grad_sink,
    )


def solution(mesh):
    placed = (
        P("dp", "seq", None),
        P("dp", "seq", None),
        P("dp", "seq", None),
        P(),
        P("dp", "seq", None),
        P(),
    )
    return jax.shard_map(
        on_device,
        mesh=mesh,
        in_specs=placed,
        out_specs=(
            P("dp", "seq", None),
            P("dp", "seq", None),
            P("dp", "seq", None),
            P("dp", "seq", None),
            P(),
        ),
        check_vma=False,
    )
```

```python
import functools

import jax
import jax.numpy as jnp
from jax import lax
from jax.experimental import pallas as pl
from jax.experimental.pallas import tpu as pltpu
from jax.sharding import PartitionSpec as P

MESH = pl.DeviceIdType.MESH

HEAD = 128
BLOCK = 128


tile_group = 4


def tile_scores(queries, key_tiles, scaling):
    return (
        jnp.einsum("gqe,gkbe->gqkb", queries, key_tiles, preferred_element_type=jnp.float32)
        * scaling
    )


def log_totals(scores, sink_value):
    row_top = jnp.maximum(jnp.max(scores, axis=(2, 3)), sink_value)
    summed = jnp.sum(jnp.exp(scores - row_top[:, :, None, None]), axis=(2, 3)) + jnp.exp(
        sink_value - row_top
    )
    return row_top + jnp.log(summed)


def softmax_weights(scores, log_total):
    weights = jnp.exp(scores - log_total[:, :, None, None])
    return (weights, weights.astype(jnp.bfloat16))


def attend(rounded, value_tiles):
    return jnp.einsum(
        "gqkb,gkbe->gqe", rounded, value_tiles, preferred_element_type=jnp.float32
    ).astype(jnp.bfloat16)


def gradients(
    weights,
    rounded,
    attended,
    queries,
    key_tiles,
    value_tiles,
    grad_tile,
    log_total,
    sink_value,
    scaling,
):
    row_dot = jnp.sum(grad_tile.astype(jnp.float32) * attended.astype(jnp.float32), axis=-1)
    grad_weights = jnp.einsum(
        "gqe,gkbe->gqkb", grad_tile, value_tiles, preferred_element_type=jnp.float32
    )
    grad_scores = (weights * (grad_weights - row_dot[:, :, None, None])).astype(jnp.bfloat16)
    grad_query = (
        jnp.einsum("gqkb,gkbe->gqe", grad_scores, key_tiles, preferred_element_type=jnp.float32)
        * scaling
    ).astype(jnp.bfloat16)
    key_part = (
        jnp.einsum("gqkb,gqe->gkbe", grad_scores, queries, preferred_element_type=jnp.float32)
        * scaling
    )
    value_part = jnp.einsum(
        "gqkb,gqe->gkbe", rounded, grad_tile, preferred_element_type=jnp.float32
    )
    sink_part = -jnp.sum(jnp.exp(sink_value - log_total) * row_dot)
    return (grad_query, key_part, value_part, sink_part)


def head_tiles(array_in, head_index):
    row_count = array_in.shape[0]
    picked = lax.dynamic_index_in_dim(array_in, head_index, 1, keepdims=False)
    return picked.reshape(row_count // BLOCK, BLOCK, HEAD)


def put_head(buffer, tiles, head_index):
    return lax.dynamic_update_slice_in_dim(buffer, tiles.reshape(-1, 1, HEAD), head_index, 1)


def group_rows(tiles, group_index):
    return lax.dynamic_slice_in_dim(tiles, group_index * tile_group, tile_group, 0)


def put_group(buffer, tiles, group_index):
    return lax.dynamic_update_slice_in_dim(buffer, tiles, group_index * tile_group, 0)


def put_scalar(buffer, value_in, head_index):
    return lax.dynamic_update_slice_in_dim(buffer, value_in[None], head_index, 0)


def forward_pass(query_heads, key_heads, value_heads, head_links, head_sinks, scaling):
    row_count, local_heads, _ = query_heads.shape
    block_count = row_count // BLOCK

    def forward_one_head(head_index, head_state):
        attended, log_total = head_state
        query_tiles = head_tiles(query_heads, head_index)
        key_all = head_tiles(key_heads, head_index)
        value_all = head_tiles(value_heads, head_index)
        link_rows = lax.dynamic_index_in_dim(head_links, head_index, 0, keepdims=False)
        sink_value = lax.dynamic_index_in_dim(head_sinks, head_index, 0, keepdims=False)

        def forward_one_group(group_index, inner_state):
            out_tiles, total_tiles = inner_state
            chosen = group_rows(link_rows, group_index)
            scores = tile_scores(group_rows(query_tiles, group_index), key_all[chosen], scaling)
            group_total = log_totals(scores, sink_value)
            _, rounded = softmax_weights(scores, group_total)
            result = attend(rounded, value_all[chosen])
            return (
                put_group(out_tiles, result, group_index),
                put_group(total_tiles, group_total, group_index),
            )

        initial = (
            jnp.zeros((block_count, BLOCK, HEAD), jnp.bfloat16),
            jnp.zeros((block_count, BLOCK), jnp.float32),
        )
        out_tiles, total_tiles = lax.fori_loop(
            0, block_count // tile_group, forward_one_group, initial
        )
        return (
            put_head(attended, out_tiles, head_index),
            lax.dynamic_update_slice_in_dim(log_total, total_tiles[None], head_index, 0),
        )

    initial = (
        jnp.zeros((row_count, local_heads, HEAD), jnp.bfloat16),
        jnp.zeros((local_heads, block_count, BLOCK), jnp.float32),
    )
    return lax.fori_loop(0, local_heads, forward_one_head, initial)


def backward_pass(
    query_heads,
    key_heads,
    value_heads,
    grad_heads,
    attended,
    log_total,
    head_links,
    head_sinks,
    scaling,
):
    row_count, local_heads, _ = query_heads.shape
    block_count = row_count // BLOCK

    def backward_one_head(head_index, head_state):
        query_grads, key_grads, value_grads, sink_terms = head_state
        query_tiles = head_tiles(query_heads, head_index)
        key_all = head_tiles(key_heads, head_index)
        value_all = head_tiles(value_heads, head_index)
        grad_tiles = head_tiles(grad_heads, head_index)
        out_tiles = head_tiles(attended, head_index)
        head_total = lax.dynamic_index_in_dim(log_total, head_index, 0, keepdims=False)
        link_rows = lax.dynamic_index_in_dim(head_links, head_index, 0, keepdims=False)
        sink_value = lax.dynamic_index_in_dim(head_sinks, head_index, 0, keepdims=False)

        def backward_one_group(group_index, inner_state):
            query_part_all, key_acc, value_acc, sink_acc = inner_state
            chosen = group_rows(link_rows, group_index)
            queries = group_rows(query_tiles, group_index)
            key_tiles = key_all[chosen]
            value_tiles = value_all[chosen]
            group_total = group_rows(head_total, group_index)
            scores = tile_scores(queries, key_tiles, scaling)
            weights, rounded = softmax_weights(scores, group_total)
            grad_query, key_part, value_part, sink_part = gradients(
                weights,
                rounded,
                group_rows(out_tiles, group_index),
                queries,
                key_tiles,
                value_tiles,
                group_rows(grad_tiles, group_index),
                group_total,
                sink_value,
                scaling,
            )
            flat_links = chosen.reshape(-1)
            key_acc = key_acc.at[flat_links].add(key_part.reshape(-1, BLOCK, HEAD))
            value_acc = value_acc.at[flat_links].add(value_part.reshape(-1, BLOCK, HEAD))
            return (
                put_group(query_part_all, grad_query, group_index),
                key_acc,
                value_acc,
                sink_acc + sink_part,
            )

        initial = (
            jnp.zeros((block_count, BLOCK, HEAD), jnp.bfloat16),
            jnp.zeros((block_count, BLOCK, HEAD), jnp.float32),
            jnp.zeros((block_count, BLOCK, HEAD), jnp.float32),
            jnp.zeros((), jnp.float32),
        )
        query_part_all, key_acc, value_acc, sink_acc = lax.fori_loop(
            0, block_count // tile_group, backward_one_group, initial
        )
        return (
            put_head(query_grads, query_part_all, head_index),
            put_head(key_grads, key_acc.astype(jnp.bfloat16), head_index),
            put_head(value_grads, value_acc.astype(jnp.bfloat16), head_index),
            put_scalar(sink_terms, sink_acc, head_index),
        )

    blank = jnp.zeros((row_count, local_heads, HEAD), jnp.bfloat16)
    initial = (blank, blank, blank, jnp.zeros((local_heads,), jnp.float32))
    return lax.fori_loop(0, local_heads, backward_one_head, initial)


def exchange_kernel(
    n,
    documents,
    local_heads,
    scaling,
    query_ref,
    key_ref,
    value_ref,
    grad_ref,
    sink_ref,
    attended_ref,
    query_grad_ref,
    key_grad_ref,
    value_grad_ref,
    sink_out_ref,
    held,
    made,
    key_acc,
    value_acc,
    sink_values,
    sink_terms,
    sink_totals,
    sink_copy,
    own_in,
    own_out,
    in_send,
    in_recv,
    out_send,
    out_recv,
    terms_send,
    terms_recv,
    totals_send,
    totals_recv,
):
    me = lax.axis_index("seq")
    document = lax.axis_index("dp")
    rows = query_ref.shape[0]
    total_rows = held.shape[2]
    given = (query_ref, key_ref, value_ref, grad_ref)
    wanted = (attended_ref, query_grad_ref, key_grad_ref, value_grad_ref)

    def partner(step):
        return lax.rem(me + step, n)

    def columns(device, head):
        return pl.ds(pl.multiple_of((device * local_heads + head) * HEAD, HEAD), HEAD)

    def row_range(device):
        return pl.ds(pl.multiple_of(device * rows, rows), rows)

    def copies_in(head, pair):
        own, remote = [], []
        for which in (2 * pair, 2 * pair + 1):
            source = given[which]
            own.append(
                pltpu.make_async_copy(
                    source.at[:, columns(me, head)],
                    held.at[which, head, row_range(me)],
                    own_in.at[head, which],
                )
            )
            for step in range(1, n):
                to = partner(step)
                remote.append(
                    pltpu.make_async_remote_copy(
                        src_ref=source.at[:, columns(to, head)],
                        dst_ref=held.at[which, head, row_range(me)],
                        send_sem=in_send.at[head, which, step - 1],
                        recv_sem=in_recv.at[head, which, step - 1],
                        device_id={"seq": to},
                        device_id_type=MESH,
                    )
                )
        return own, remote

    def own_copy(which, head):
        return pltpu.make_async_copy(
            made.at[which, head, row_range(me)],
            wanted[which].at[:, columns(me, head)],
            own_out.at[head, which],
        )

    def copy_out(which, head, step):
        to = partner(step)
        return pltpu.make_async_remote_copy(
            src_ref=made.at[which, head, row_range(to)],
            dst_ref=wanted[which].at[:, columns(me, head)],
            send_sem=out_send.at[head, which, step - 1],
            recv_sem=out_recv.at[head, which, step - 1],
            device_id={"seq": to},
            device_id_type=MESH,
        )

    def start_all(copies):
        own, remote = copies
        for copy in remote + own:
            copy.start()

    def terms_copies():
        return [
            pltpu.make_async_remote_copy(
                src_ref=sink_terms.at[document],
                dst_ref=sink_terms.at[document],
                send_sem=terms_send.at[step - 1],
                recv_sem=terms_recv.at[step - 1],
                device_id={"dp": lax.rem(document + step, documents)},
                device_id_type=MESH,
            )
            for step in range(1, documents)
        ]

    def totals_copies():
        return [
            pltpu.make_async_remote_copy(
                src_ref=sink_totals.at[me],
                dst_ref=sink_totals.at[me],
                send_sem=totals_send.at[step - 1],
                recv_sem=totals_recv.at[step - 1],
                device_id={"seq": partner(step)},
                device_id_type=MESH,
            )
            for step in range(1, n)
        ]

    sinks_in = pltpu.make_async_copy(sink_ref, sink_values, sink_copy)
    sinks_in.start()
    barrier = pltpu.get_barrier_semaphore()
    for step in range(1, n):
        pl.semaphore_signal(
            barrier, inc=1, device_id={"seq": partner(step)}, device_id_type=MESH
        )
    for step in range(1, documents):
        other = lax.rem(document + step, documents)
        pl.semaphore_signal(barrier, inc=1, device_id={"dp": other}, device_id_type=MESH)
    pl.semaphore_wait(barrier, n + documents - 2)

    start_all(copies_in(0, 0))
    start_all(copies_in(0, 1))
    sink_terms[document] = jnp.zeros(sink_out_ref.shape, jnp.float32)
    lanes = lax.broadcasted_iota(jnp.int32, sink_out_ref.shape, 1)
    sinks_in.wait()

    def one_head(head, carry):
        for pair in range(2):
            own, remote = copies_in(head, pair)
            for copy in own:
                copy.wait()
            for copy in remote:
                copy.wait_recv()

            if pair == 0 and local_heads > 1:

                @pl.when(head == 0)
                def _():
                    start_all(copies_in(1, 0))

        @pl.when(head + 1 < local_heads)
        def _():
            start_all(copies_in(head + 1, 1))

        @pl.when(head + 2 < local_heads)
        def _():
            start_all(copies_in(head + 2, 0))

        sink_value = sink_values[me * local_heads + head]
        key_acc[...] = jnp.zeros_like(key_acc)
        value_acc[...] = jnp.zeros_like(value_acc)

        def one_chunk(step, sink_sum):
            part = row_range(partner(step))
            queries = held[0, head, part]
            keys = held[1, head]
            values = held[2, head]
            grads = held[3, head, part]
            scores = dot(queries, keys, 1, 1) * scaling
            row_top = jnp.maximum(jnp.max(scores, axis=1, keepdims=True), sink_value)
            raised = jnp.exp(scores - row_top)
            sink_raised = jnp.exp(sink_value - row_top)
            inverse = 1.0 / (jnp.sum(raised, axis=1, keepdims=True) + sink_raised)
            weights = raised * inverse
            rounded = weights.astype(jnp.bfloat16)
            attended = dot(rounded, values, 1, 0).astype(jnp.bfloat16)
            made[0, head, part] = attended
            row_dot = jnp.sum(
                grads.astype(jnp.float32) * attended.astype(jnp.float32), axis=1, keepdims=True
            )
            grad_weights = dot(grads, values, 1, 1)
            grad_scores = (weights * (grad_weights - row_dot)).astype(jnp.bfloat16)
            made[1, head, part] = (dot(grad_scores, keys, 1, 0) * scaling).astype(jnp.bfloat16)

            @pl.when(step < n)
            def _():
                for which in range(2):
                    copy_out(which, head, step).start()

            value_acc[...] += dot(rounded, grads, 0, 0)
            key_acc[...] += dot(grad_scores, queries, 0, 0)
            terms = sink_raised * inverse * row_dot
            return sink_sum + jnp.sum(terms, axis=0, keepdims=True)

        sink_sum = lax.fori_loop(
            1, n + 1, one_chunk, jnp.zeros((1, 1), jnp.float32)
        )
        made[2, head] = (key_acc[...] * scaling).astype(jnp.bfloat16)
        made[3, head] = value_acc[...].astype(jnp.bfloat16)
        sink_terms[document] = jnp.where(
            lanes == me * local_heads + head, -sink_sum, sink_terms[document]
        )

        @pl.when(head == local_heads - 1)
        def _():
            for copy in terms_copies():
                copy.start()

        for which in range(2, 4):
            for step in range(1, n):
                copy_out(which, head, step).start()
        for which in range(4):
            own_copy(which, head).start()
        return carry

    lax.fori_loop(0, local_heads, one_head, 0)

    for copy in terms_copies():
        copy.wait()
    sink_totals[me] = jnp.sum(sink_terms[...], axis=0)
    for copy in totals_copies():
        copy.start()
    for copy in totals_copies():
        copy.wait()
    sink_out_ref[...] = jnp.sum(sink_totals[...], axis=0) * (1.0 / documents)

    def finish(head, carry):
        for pair in range(2):
            for copy in copies_in(head, pair)[1]:
                copy.wait_send()
        for which in range(4):
            own_copy(which, head).wait()
            for step in range(1, n):
                copy_out(which, head, step).wait()
        return carry

    lax.fori_loop(0, local_heads, finish, 0)


def store_kernel(*refs):
    sources, sink_ref, targets, sink_out_ref, done = refs[:4], refs[4], refs[5:9], refs[9], refs[10]
    rows = sources[0].shape[0] // 4
    copies = [
        pltpu.make_async_copy(
            source.at[pl.ds(half * rows, rows)],
            target.at[pl.ds(half * rows, rows)],
            done.at[which, half],
        )
        for which, (source, target) in enumerate(zip(sources, targets))
        for half in range(4)
    ]
    for copy in copies:
        copy.start()
    sink_out_ref[...] = sink_ref[0, : sink_out_ref.shape[0]]
    for copy in copies:
        copy.wait()


def dot(left, right, left_dim, right_dim):
    return lax.dot_general(
        left,
        right,
        (((left_dim,), (right_dim,)), ((), ())),
        preferred_element_type=jnp.float32,
    )


def every_block(query_rows, key_rows, value_rows, sink_logit, grad_out):
    token_count = query_rows.shape[1]
    head_count = sink_logit.shape[0]
    n = lax.axis_size("seq")
    local_heads = head_count // n
    total_rows = n * token_count
    width = head_count * HEAD
    documents = lax.axis_size("dp")
    anywhere = pl.BlockSpec(memory_space=pl.ANY)
    in_hbm = pl.BlockSpec(memory_space=pltpu.HBM)
    in_vmem = pl.BlockSpec(memory_space=pltpu.VMEM)
    result = jax.ShapeDtypeStruct((token_count, width), jnp.bfloat16)
    outs = pl.pallas_call(
        functools.partial(exchange_kernel, n, documents, local_heads, HEAD ** (-0.5)),
        out_shape=(result,) * 4 + (jax.ShapeDtypeStruct((8, 128), jnp.float32),),
        in_specs=[in_hbm] * 5,
        out_specs=(anywhere,) * 4 + (in_vmem,),
        scratch_shapes=[
            pltpu.VMEM((4, local_heads, total_rows, HEAD), jnp.bfloat16),
            pltpu.VMEM((4, local_heads, total_rows, HEAD), jnp.bfloat16),
            pltpu.VMEM((total_rows, HEAD), jnp.float32),
            pltpu.VMEM((total_rows, HEAD), jnp.float32),
            pltpu.SMEM((head_count,), jnp.float32),
            pltpu.VMEM((documents, 8, 128), jnp.float32),
            pltpu.VMEM((n, 8, 128), jnp.float32),
            pltpu.SemaphoreType.DMA,
            pltpu.SemaphoreType.DMA((local_heads, 4)),
            pltpu.SemaphoreType.DMA((local_heads, 4)),
            pltpu.SemaphoreType.DMA((local_heads, 4, n - 1)),
            pltpu.SemaphoreType.DMA((local_heads, 4, n - 1)),
            pltpu.SemaphoreType.DMA((local_heads, 4, n - 1)),
            pltpu.SemaphoreType.DMA((local_heads, 4, n - 1)),
            pltpu.SemaphoreType.DMA((documents - 1,)),
            pltpu.SemaphoreType.DMA((documents - 1,)),
            pltpu.SemaphoreType.DMA((n - 1,)),
            pltpu.SemaphoreType.DMA((n - 1,)),
        ],
        compiler_params=pltpu.CompilerParams(
            collective_id=0, has_side_effects=True, vmem_limit_bytes=49 * 1024 * 1024
        ),
        cost_estimate=pl.CostEstimate(
            flops=12 * local_heads * total_rows * total_rows * HEAD,
            bytes_accessed=16 * token_count * width,
            transcendentals=local_heads * total_rows * total_rows,
        ),
    )(
        query_rows.reshape(token_count, width),
        key_rows.reshape(token_count, width),
        value_rows.reshape(token_count, width),
        grad_out.reshape(token_count, width),
        sink_logit,
    )
    stored = pl.pallas_call(
        store_kernel,
        out_shape=(result,) * 4 + (jax.ShapeDtypeStruct((head_count,), jnp.float32),),
        in_specs=[anywhere] * 4 + [in_vmem],
        out_specs=(in_hbm,) * 4 + (in_vmem,),
        scratch_shapes=[pltpu.SemaphoreType.DMA((4, 4))],
        compiler_params=pltpu.CompilerParams(vmem_limit_bytes=4 * 1024 * 1024),
    )(*outs)
    return tuple(out[None] for out in stored[:4]) + (stored[4],)


def on_device(query_rows, key_rows, value_rows, sink_logit, grad_out, pattern):
    if pattern.shape[1] == pattern.shape[2]:
        return every_block(query_rows, key_rows, value_rows, sink_logit, grad_out)
    token_count = query_rows.shape[1]
    head_count = sink_logit.shape[0]
    local_heads = head_count // lax.axis_size("seq")
    first_head = lax.axis_index("seq") * local_heads
    head_links = lax.dynamic_slice_in_dim(pattern, first_head, local_heads, 0)
    head_sinks = lax.dynamic_slice_in_dim(sink_logit, first_head, local_heads, 0)
    scaling = HEAD ** (-0.5)

    def split_heads(array_in):
        return array_in.reshape(token_count, head_count, HEAD)

    def join_heads(array_in):
        return array_in.reshape(1, token_count, head_count * HEAD)

    query_heads, key_heads, value_heads = (
        lax.all_to_all(split_heads(query_rows), "seq", split_axis=1, concat_axis=0, tiled=True),
        lax.all_to_all(split_heads(key_rows), "seq", split_axis=1, concat_axis=0, tiled=True),
        lax.all_to_all(split_heads(value_rows), "seq", split_axis=1, concat_axis=0, tiled=True),
    )
    attended_heads, log_total = forward_pass(
        query_heads, key_heads, value_heads, head_links, head_sinks, scaling
    )
    attended = lax.all_to_all(attended_heads, "seq", split_axis=0, concat_axis=1, tiled=True)
    grad_heads = lax.all_to_all(
        split_heads(grad_out), "seq", split_axis=1, concat_axis=0, tiled=True
    )
    query_grads, key_grads, value_grads, sink_terms = backward_pass(
        query_heads,
        key_heads,
        value_heads,
        grad_heads,
        attended_heads,
        log_total,
        head_links,
        head_sinks,
        scaling,
    )
    grad_query, grad_key, grad_value = (
        lax.all_to_all(query_grads, "seq", split_axis=0, concat_axis=1, tiled=True),
        lax.all_to_all(key_grads, "seq", split_axis=0, concat_axis=1, tiled=True),
        lax.all_to_all(value_grads, "seq", split_axis=0, concat_axis=1, tiled=True),
    )
    spread = lax.dynamic_update_slice_in_dim(
        jnp.zeros((head_count,), jnp.float32), sink_terms, first_head, 0
    )
    summed = lax.psum(spread, ("seq", "dp"))
    grad_sink = summed / lax.axis_size("dp")
    return (
        join_heads(attended),
        join_heads(grad_query),
        join_heads(grad_key),
        join_heads(grad_value),
        grad_sink,
    )


def solution(mesh):
    placed = (
        P("dp", "seq", None),
        P("dp", "seq", None),
        P("dp", "seq", None),
        P(),
        P("dp", "seq", None),
        P(),
    )
    return jax.shard_map(
        on_device,
        mesh=mesh,
        in_specs=placed,
        out_specs=(
            P("dp", "seq", None),
            P("dp", "seq", None),
            P("dp", "seq", None),
            P("dp", "seq", None),
            P(),
        ),
        check_vma=False,
    )
```
